32 devices in a mesh: groups: 2 (over x), mp: 16 (over z, y, core).
Axes of the slice: x: 2, y: 2, z: 4, core: 2. Of those that a mesh axis runs over, the one named last changes fastest.
Arguments:
- acts: bfloat16 [8, 8192, 512], P('groups', 'mp'), parts along dimension 0, may hold values from -6 to 6
- output_gradients: bfloat16 [8, 8192, 512], P('groups', 'mp'), parts along dimension 0, may hold values from -6 to 6
- adapter_down: bfloat16 [128, 8192], P(None, 'mp'), may hold values from -0.0625 to 0.0625
- adapter_up: bfloat16 [8192, 128], P('mp'), may hold values from -0.0625 to 0.0625
- lengths: int32 [8], P('groups'), parts along dimension 0, may hold values from 128 to 512, as said below
- sign_hash_seed: int32 [1], replicated, may hold values from 0 to 1073741823
- tile_indices: int32 [8192], P('mp'), may hold values from 0 to 8191, each once
- validation_projected: float32 [512, 8192], P('groups', 'mp'), parts along dimension 0, may hold values from -6 to 6
Outputs:
- unit_grads: float32 [8, 8192], P('groups', 'mp'), parts along dimension 0
- alignment: float32 [8, 256], P('groups'), parts along dimension 0
- task_score: float32 [8, 4], P('groups'), parts along dimension 0
The draws below stay inside these ranges and needn't reach their ends.
There are 2 independent parts, one for each index of `groups`. The reference program is written for one: setup_inputs(seed, part) draws one part's arguments, and reference() takes and returns one part's arrays. A program takes and returns all parts, laid end to end along the dimension named above; an argument that names none is the same for every part. Nothing has to cross between parts.
Inputs may be any that keep to these rules, and one draw needn't show every extreme that they name: `lengths`: every example keeps a quarter of 512 or more tokens; one example of every group is full length. `tile_indices`: a permutation of the row numbers.
All inputs are finite; a program needn't handle non-finite values.
Results may differ from the reference program's by a relative error of at most 0.0046.
Values may be sent and summed in bfloat16 or wider, within the bound.
No kernel may reach another device: no remote copies, remote signals or barrier semaphores. Data moves between devices by JAX's collectives and lax.ppermute only.
A program may use at most 64 MiB of HBM per device.

```python
import math
import jax
import jax.numpy as jnp
from jax import lax

MODEL_WIDTH = 8192
ADAPTER_RANK = 128
PROJECTED_DIMS = 8192
S = 512
EX = 4
TASKS = 4
PER_TASK = 64
NVAL = 256


def draw_lengths(key, part):
    key = jax.random.fold_in(key, 7)
    length_key, chosen_key = jax.random.split(key)
    drawn = jax.random.randint(length_key, (EX,), S // 4, S + 1, dtype=jnp.int32)
    chosen = jax.random.randint(chosen_key, (), 0, EX, dtype=jnp.int32)
    return jnp.where(jnp.arange(EX, dtype=jnp.int32) == chosen, jnp.int32(S), drawn).astype(jnp.int32)


def block_scale(key, extent, cuts, smallest, high):
    def one(position, blocks):
        heights = jax.random.uniform(jax.random.fold_in(jax.random.fold_in(key, 6), position), (blocks,), jnp.float32, smallest / len(cuts), high / len(cuts))
        return jnp.repeat(jnp.exp(heights), extent[position] // blocks).reshape((-1,) + (1,) * (len(extent) - position - 1))

    loudness = one(*cuts[0])
    for cut in cuts[1:]:
        loudness = loudness * one(*cut)
    return loudness


def noise(rng, shape, scale, bound, cuts=(), kind=jnp.bfloat16):
    gain = block_scale(rng, shape, cuts, -0.22, 0.18) if cuts else 1.0
    entries = jax.random.normal(rng, shape, jnp.float32) * scale * gain
    return jnp.minimum(jnp.maximum(entries, -bound), bound).astype(kind)


def setup_inputs(seed: int = 0, part: int = 0) -> dict:
    keys = jax.random.split(jax.random.key(seed), 9)
    own_keys = jax.random.split(jax.random.fold_in(keys[8], part), 9)
    return {
        "acts": noise(own_keys[0], (EX, MODEL_WIDTH, S), 1.0, 6.0, ((1, 16),)),
        "output_gradients": noise(own_keys[1], (EX, MODEL_WIDTH, S), 1.0, 6.0, ((1, 16),)),
        "adapter_down": noise(keys[2], (ADAPTER_RANK, MODEL_WIDTH), MODEL_WIDTH ** -0.5, 0.0625, ((1, 16),)),
        "adapter_up": noise(keys[3], (MODEL_WIDTH, ADAPTER_RANK), MODEL_WIDTH ** -0.5, 0.0625, ((0, 16),)),
        "lengths": draw_lengths(jax.random.fold_in(jax.random.fold_in(keys[8], part), 71), part),
        "sign_hash_seed": jax.random.randint(keys[5], (1,), 0, 1073741824).astype(jnp.int32),
        "tile_indices": jax.random.permutation(keys[6], MODEL_WIDTH).astype(jnp.int32),
        "validation_projected": noise(own_keys[7], (NVAL, PROJECTED_DIMS), 1.0, 6.0, ((1, 16),), jnp.float32),
    }


def scramble(hashed):
    hashed = hashed ^ lax.shift_right_logical(hashed, jnp.full_like(hashed, 16))
    hashed = hashed * jnp.int32(2146121005)
    hashed = hashed ^ lax.shift_right_logical(hashed, jnp.full_like(hashed, 15))
    hashed = hashed * jnp.int32(-2073254261)
    hashed = hashed ^ lax.shift_right_logical(hashed, jnp.full_like(hashed, 16))
    return hashed

def sign_block(block_seeds, projected_begin, projected_count, span_width):
    groups = span_width // 32
    count_of_rows = block_seeds.shape[0]
    group_ids = lax.broadcasted_iota(jnp.int32, (1, groups, projected_count), 1)
    columns = lax.broadcasted_iota(jnp.int32, (1, groups, projected_count), 2) + projected_begin
    hash_words = scramble(block_seeds[:, None, None] + group_ids * PROJECTED_DIMS + columns)
    shifts = lax.broadcasted_iota(jnp.int32, (count_of_rows, groups, 32, projected_count), 2)
    spread = jnp.broadcast_to(hash_words[:, :, None, :], (count_of_rows, groups, 32, projected_count))
    bit_values = lax.shift_right_logical(spread, shifts) & 1
    sign_tile = (1.0 - 2.0 * bit_values.astype(jnp.float32)).astype(jnp.bfloat16)
    return sign_tile.reshape(count_of_rows, span_width, projected_count)

def reference(acts, output_gradients, adapter_down, adapter_up, lengths, sign_hash_seed, tile_indices, validation_projected):
    live_mask = jnp.arange(S, dtype=jnp.int32)[None, :] < lengths[:, None]
    masked_values = jnp.where(live_mask[:, None, :], output_gradients, jnp.zeros_like(output_gradients))
    activation_span = acts.astype(jnp.float32)
    masked_span = masked_values.astype(jnp.float32)
    adapter_input = jnp.einsum('mwx,tw->mxt', activation_span, adapter_down.astype(jnp.float32))
    adapter_output = jnp.einsum('vwx,wi->vxi', masked_span, adapter_up.astype(jnp.float32))
    adapter_hidden = jnp.concatenate([adapter_output, adapter_input], 2).astype(jnp.bfloat16)
    adapter_hidden = lax.optimization_barrier(adapter_hidden).astype(jnp.float32)
    down_gradient = jnp.einsum('xqf,xfk->xqk', activation_span, adapter_hidden[:, :, :ADAPTER_RANK])
    up_gradient = jnp.einsum('xqf,xfk->xqk', masked_span, adapter_hidden[:, :, ADAPTER_RANK:])
    adapter_gradients = jnp.concatenate([down_gradient, up_gradient], 2).astype(jnp.bfloat16)
    adapter_gradients = lax.optimization_barrier(adapter_gradients).astype(jnp.float32)
    seeds_per_row = scramble(tile_indices + scramble(sign_hash_seed[0]))
    block_of_rows = math.gcd(MODEL_WIDTH, 32)

    def add_block(running, leading_row):
        block_seeds = lax.dynamic_slice_in_dim(seeds_per_row, leading_row, block_of_rows, 0)
        gradient_portion = lax.dynamic_slice_in_dim(adapter_gradients, leading_row, block_of_rows, 1)
        sign_tile = sign_block(block_seeds, 0, PROJECTED_DIMS, 2 * ADAPTER_RANK).astype(jnp.float32)
        product = jnp.dot(gradient_portion.reshape(EX, block_of_rows * 2 * ADAPTER_RANK), sign_tile.reshape(block_of_rows * 2 * ADAPTER_RANK, PROJECTED_DIMS), precision=lax.Precision.HIGHEST)
        return (running + product, None)
    starts = jnp.arange(0, MODEL_WIDTH, block_of_rows, dtype=jnp.int32)
    projected, _ = lax.scan(add_block, jnp.zeros((EX, PROJECTED_DIMS), jnp.float32), starts)
    train_norm = jnp.sqrt(lax.optimization_barrier(jnp.sum(projected * projected, 1)) + 1e-06)
    val_norm = jnp.sqrt(lax.optimization_barrier(jnp.sum(validation_projected * validation_projected, 1)) + 1e-06)
    factor = math.sqrt(PROJECTED_DIMS)
    unit_grads = factor * projected / train_norm[:, None]
    inner_products = jnp.dot(projected, validation_projected.T, precision=lax.Precision.HIGHEST)
    alignment = factor * inner_products / (train_norm[:, None] * val_norm[None, :])
    task_score = lax.optimization_barrier(jnp.mean(alignment.reshape(EX, TASKS, PER_TASK), 2))
    return (unit_grads, alignment, task_score)
```

```python
import functools
import math

import jax
import jax.numpy as jnp
from jax import lax
from jax.experimental import pallas as pl
from jax.experimental.pallas import tpu as pltpu
from jax.sharding import PartitionSpec as P

PROJECTED_DIMS = 8192
TASKS = 4
DIGITS = 8
DIGIT_STEP = 16.0
DIGIT_TOP = 8.0
F8 = jnp.float8_e4m3fn
SPANS = ((0, 0, 64), (0, 64, 64), (1, 0, 128))


def scramble(hashed):
    hashed = hashed ^ lax.shift_right_logical(hashed, jnp.full_like(hashed, 16))
    hashed = hashed * jnp.int32(2146121005)
    hashed = hashed ^ lax.shift_right_logical(hashed, jnp.full_like(hashed, 15))
    hashed = hashed * jnp.int32(-2073254261)
    hashed = hashed ^ lax.shift_right_logical(hashed, jnp.full_like(hashed, 16))
    return hashed


def whole(shape):
    return pl.BlockSpec(shape, lambda *_: (0,) * len(shape))


def hidden_kernel(masked, lengths_ref, weight_ref, values_ref, *out_refs):
    example = pl.program_id(0)
    product = jnp.dot(weight_ref[...], values_ref[0], preferred_element_type=jnp.float32)
    if masked:
        positions = lax.broadcasted_iota(jnp.int32, product.shape, 1)
        product = jnp.where(positions < lengths_ref[example], product, 0.0)
    begin = 0
    for out_ref in out_refs:
        out_ref[0] = product[begin : begin + out_ref.shape[1]]
        begin += out_ref.shape[1]


def partial_hidden(values, weight, lengths, counts, masked):
    examples, width, tokens = values.shape
    return pl.pallas_call(
        functools.partial(hidden_kernel, masked),
        grid=(examples,),
        in_specs=[
            pl.BlockSpec(memory_space=pltpu.SMEM),
            whole(weight.shape),
            pl.BlockSpec((1, width, tokens), lambda e: (e, 0, 0)),
        ],
        out_specs=[pl.BlockSpec((1, n, tokens), lambda e: (e, 0, 0)) for n in counts],
        out_shape=[jax.ShapeDtypeStruct((examples, n, tokens), jnp.float32) for n in counts],
        name="partial_hidden",
    )(lengths, weight, values)


def grads_kernel(masked, lengths_ref, place_ref, hidden_ref, values_ref, own_ref, other_ref):
    example = pl.program_id(0)
    rows = own_ref.shape[2]
    hidden = hidden_ref[0]
    if masked:
        positions = lax.broadcasted_iota(jnp.int32, hidden.shape, 1)
        hidden = jnp.where(positions < lengths_ref[example], hidden, jnp.zeros_like(hidden))
    mine = place_ref[0]
    for out_ref, half in ((own_ref, mine), (other_ref, 1 - mine)):
        values = values_ref[0, pl.ds(pl.multiple_of(half * rows, rows), rows), :]
        out_ref[0] = lax.dot_general(
            hidden, values, (((1,), (1,)), ((), ())), preferred_element_type=jnp.float32
        ).astype(jnp.bfloat16)


def gradients(hidden, values, lengths, place, masked):
    examples, columns, tokens = hidden.shape
    width = values.shape[1]
    shape = (examples, columns, width // 2)
    return pl.pallas_call(
        functools.partial(grads_kernel, masked),
        grid=(examples,),
        in_specs=[
            pl.BlockSpec(memory_space=pltpu.SMEM),
            pl.BlockSpec(memory_space=pltpu.SMEM),
            pl.BlockSpec((1, columns, tokens), lambda e: (e, 0, 0)),
            pl.BlockSpec((1, width, tokens), lambda e: (e, 0, 0)),
        ],
        out_specs=[pl.BlockSpec((1,) + shape[1:], lambda e: (e, 0, 0))] * 2,
        out_shape=[jax.ShapeDtypeStruct(shape, jnp.bfloat16)] * 2,
        name="gradients",
    )(lengths, place, hidden, values)


def digits_kernel(place_ref, own_ref, other_ref, digits_ref, scale_ref, turned):
    first = place_ref[0] == 0
    own, other = own_ref[...].astype(jnp.float32), other_ref[...].astype(jnp.float32)
    examples = own.shape[0]
    for e in range(examples):
        turned[:, e, :] = jnp.where(first, own[e], other[e])
        turned[:, examples + e, :] = jnp.where(first, other[e], own[e])
    values = turned[...]
    largest = jnp.max(jnp.max(jnp.abs(values), axis=0), axis=1, keepdims=True)
    largest = jnp.maximum(largest, 1e-30)
    rest = values * (DIGIT_TOP / largest)[None]
    digits = []
    for _ in range(DIGITS):
        digit = jnp.round(rest)
        digits.append(digit)
        rest = (rest - digit) * DIGIT_STEP
    digits_ref[...] = jnp.concatenate(digits, axis=1).astype(F8)
    scale_ref[...] = largest * (1 / DIGIT_TOP)


def split_digits(own, received, place):
    examples, columns, rows = own.shape
    lines = 2 * examples
    return pl.pallas_call(
        digits_kernel,
        grid=(1,),
        in_specs=[pl.BlockSpec(memory_space=pltpu.SMEM), whole(own.shape), whole(own.shape)],
        out_specs=[whole((columns, DIGITS * lines, rows)), whole((lines, 1))],
        out_shape=[
            jax.ShapeDtypeStruct((columns, DIGITS * lines, rows), F8),
            jax.ShapeDtypeStruct((lines, 1), jnp.float32),
        ],
        scratch_shapes=[pltpu.VMEM((columns, lines, rows), jnp.float32)],
        compiler_params=pltpu.CompilerParams(vmem_limit_bytes=48 << 20),
        name="split_digits",
    )(place, own, received)


def project_kernel(first_group, seeds_ref, digits_ref, scale_ref, before_ref, out_ref, total):
    block, group = pl.program_id(0), pl.program_id(1)
    count = total.shape[1]
    rows = seeds_ref.shape[0]
    begin = (first_group + group) * PROJECTED_DIMS + block * count

    @pl.when(group == 0)
    def _():
        total[...] = jnp.zeros_like(total)

    columns = lax.broadcasted_iota(jnp.int32, (rows, count), 1)
    words = scramble((seeds_ref[...] + begin) + columns)
    signs = []
    for byte in range(4):
        shifted = lax.shift_right_logical(words, jnp.full_like(words, 8 * byte)) if byte else words
        shifted = shifted.astype(jnp.int8)
        for bit in range(8):
            mask = jnp.int8((1 << bit) - 256 * (bit == 7))
            signs.append(jnp.where((shifted & mask) != 0, F8(-1), F8(1)))
    digits = jnp.concatenate([digits_ref[c] for c in range(32)], axis=1)
    total[...] += jnp.dot(
        digits, jnp.concatenate(signs, axis=0), preferred_element_type=jnp.float32
    )

    @pl.when(group == pl.num_programs(1) - 1)
    def _():
        examples = out_ref.shape[0]
        added = total[(DIGITS - 1) * examples :, :]
        for digit in reversed(range(DIGITS - 1)):
            added = added * (1 / DIGIT_STEP) + total[digit * examples : (digit + 1) * examples, :]
        out_ref[...] = before_ref[...] + added * scale_ref[...]


def project(seeds, digits, scale, before, first_group):
    rows = seeds.shape[0]
    columns, lines, _ = digits.shape
    examples = scale.shape[0]
    count = 2048
    return pl.pallas_call(
        functools.partial(project_kernel, first_group),
        grid=(PROJECTED_DIMS // count, columns // 32),
        in_specs=[
            whole((rows, 1)),
            pl.BlockSpec((32, lines, rows), lambda k, g: (g, 0, 0)),
            whole((examples, 1)),
            pl.BlockSpec((examples, count), lambda k, g: (0, k)),
        ],
        out_specs=pl.BlockSpec((examples, count), lambda k, g: (0, k)),
        out_shape=jax.ShapeDtypeStruct((examples, PROJECTED_DIMS), jnp.float32),
        scratch_shapes=[pltpu.VMEM((lines, count), jnp.float32)],
        cost_estimate=pl.CostEstimate(
            flops=2 * 256 * columns * rows * PROJECTED_DIMS, bytes_accessed=digits.size, transcendentals=0
        ),
        compiler_params=pltpu.CompilerParams(vmem_limit_bytes=48 << 20),
        name="project",
    )(seeds, digits, scale, before)


def shards(
    acts,
    output_gradients,
    adapter_down,
    adapter_up,
    lengths,
    sign_hash_seed,
    tile_indices,
    validation_projected,
    parts=2,
    devices=16,
):
    examples, width, tokens = acts.shape
    group = lax.axis_index("groups")
    place = group.astype(jnp.int32).reshape(1)

    terms = {}
    for half, (values, weight) in enumerate(((output_gradients, adapter_up.T), (acts, adapter_down))):
        spans = [s for s in SPANS if s[0] == half]
        found = partial_hidden(values, weight, lengths, [s[2] for s in spans], half == 0)
        terms.update(zip(spans, found))

    row_seeds = scramble(tile_indices + scramble(sign_hash_seed[0]))
    row_seeds = lax.dynamic_slice_in_dim(row_seeds, group * (width // 2), width // 2, 0)[:, None]

    projected = jnp.zeros((parts * examples, PROJECTED_DIMS), jnp.float32)
    for span in SPANS:
        half, begin, count = span
        rows = examples * count // devices
        sent = terms[span].reshape(devices, rows, tokens)
        summed = lax.all_to_all(sent, "mp", 0, 0, tiled=True).sum(0).astype(jnp.bfloat16)
        hidden = lax.all_to_all(
            jnp.broadcast_to(summed[None], (devices, rows, tokens)), "mp", 0, 0, tiled=True
        ).reshape(examples, count, tokens)
        values = output_gradients if half else acts
        own, other = gradients(hidden, values, lengths, place, half == 1)
        received = lax.ppermute(other, "groups", [(0, 1), (1, 0)])
        digits, scale = split_digits(own, received, place)
        projected = project(row_seeds, digits, scale, projected, (half * adapter_down.shape[0] + begin) // 32)

    local_k = validation_projected.shape[1]
    sent = projected.reshape(parts, examples, devices, local_k).transpose(0, 2, 1, 3)
    sent = sent.reshape(parts * devices, examples, local_k)
    own = lax.all_to_all(sent, ("groups", "mp"), 0, 0, tiled=True).sum(0)

    inner = jnp.einsum("ek,vk->ev", own, validation_projected, precision=lax.Precision.HIGHEST)
    val_sq = jnp.sum(validation_projected * validation_projected, 1)
    train_sq = jnp.sum(own * own, 1)
    packed = jnp.concatenate(
        [inner, val_sq[None, :], jnp.pad(train_sq, (0, inner.shape[1] - examples))[None, :]], 0
    )
    packed = jnp.pad(packed, ((0, -packed.shape[0] % 8), (0, 0)))
    summed = lax.all_to_all(
        jnp.broadcast_to(packed[None], (devices,) + packed.shape), "mp", 0, 0, tiled=True
    ).sum(0)
    train_norm = jnp.sqrt(summed[examples + 1, :examples] + 1e-06)
    val_norm = jnp.sqrt(summed[examples] + 1e-06)
    factor = math.sqrt(PROJECTED_DIMS)
    unit_grads = own * (factor / train_norm)[:, None]
    alignment = factor * summed[:examples] / (train_norm[:, None] * val_norm[None, :])
    task_score = jnp.mean(alignment.reshape(examples, TASKS, -1), 2)
    return (unit_grads, alignment, task_score)


def solution(mesh):
    placed = (
        P("groups", "mp", None),
        P("groups", "mp", None),
        P(None, "mp"),
        P("mp", None),
        P("groups"),
        P(),
        P("mp"),
        P("groups", "mp"),
    )
    return jax.shard_map(
        functools.partial(shards, parts=mesh.shape["groups"], devices=mesh.shape["mp"]),
        mesh=mesh,
        in_specs=placed,
        out_specs=(P("groups", "mp"), P("groups", None), P("groups", None)),
        check_vma=False,
    )
```

```python
import functools
import math

import jax
import jax.numpy as jnp
from jax import lax
from jax.experimental import pallas as pl
from jax.experimental.pallas import tpu as pltpu
from jax.sharding import Mesh
from jax.sharding import PartitionSpec as P

PROJECTED_DIMS = 8192
TASKS = 4
DIGITS = 4
DIGIT_STEP = 16.0
DIGIT_TOP = 8.0
F8 = jnp.float8_e4m3fn
PROJECTED_BLOCK = 2048


def scramble(hashed):
    hashed = hashed ^ lax.shift_right_logical(hashed, jnp.full_like(hashed, 16))
    hashed = hashed * jnp.int32(2146121005)
    hashed = hashed ^ lax.shift_right_logical(hashed, jnp.full_like(hashed, 15))
    hashed = hashed * jnp.int32(-2073254261)
    hashed = hashed ^ lax.shift_right_logical(hashed, jnp.full_like(hashed, 16))
    return hashed


def whole(shape):
    return pl.BlockSpec(shape, lambda *_: (0,) * len(shape))


def after(value, earlier):
    return pl.pallas_call(
        lambda value_ref, earlier_ref, out_ref: None,
        in_specs=[pl.BlockSpec(memory_space=pl.ANY), whole(earlier.shape)],
        out_specs=pl.BlockSpec(memory_space=pl.ANY),
        out_shape=jax.ShapeDtypeStruct(value.shape, value.dtype),
        input_output_aliases={0: 0},
        grid=(1,),
        name="after",
    )(value, earlier)


def hidden_kernel(masked, weight_dim, order_ref, lengths_ref, weight_ref, values_ref, earlier_ref, sent_ref, kept_ref, done_ref):
    step = pl.program_id(0)
    product = lax.dot_general(
        weight_ref[...], values_ref[0], (((weight_dim,), (0,)), ((), ())), preferred_element_type=jnp.float32
    )
    if masked:
        positions = lax.broadcasted_iota(jnp.int32, product.shape, 1)
        product = jnp.where(positions < lengths_ref[order_ref[step]], product, 0.0)
    early = step < sent_ref.shape[0] * (pl.num_programs(0) // 2)

    @pl.when(early)
    def _():
        sent_ref[0] = product

    @pl.when(jnp.logical_not(early))
    def _():
        kept_ref[0] = product

    done_ref[...] = earlier_ref[...]


def partial_hidden(values, weight, lengths, order, masked, earlier):
    examples, width, tokens = values.shape
    weight_dim = 0 if masked else 1
    count = weight.shape[1 - weight_dim]
    half = examples // 2
    shape = jax.ShapeDtypeStruct((half, count, tokens), jnp.float32)
    return pl.pallas_call(
        functools.partial(hidden_kernel, masked, weight_dim),
        grid_spec=pltpu.PrefetchScalarGridSpec(
            num_scalar_prefetch=1,
            grid=(examples,),
            in_specs=[
                pl.BlockSpec(memory_space=pltpu.SMEM),
                whole(weight.shape),
                pl.BlockSpec((1, width, tokens), lambda e, order: (order[e], 0, 0)),
                whole(earlier.shape),
            ],
            out_specs=[
                pl.BlockSpec((1, count, tokens), lambda e, order: (jnp.minimum(e, half - 1), 0, 0)),
                pl.BlockSpec((1, count, tokens), lambda e, order: (jnp.maximum(e - half, 0), 0, 0)),
                whole(earlier.shape),
            ],
        ),
        out_shape=[shape, shape, jax.ShapeDtypeStruct(earlier.shape, earlier.dtype)],
        name="partial_hidden",
    )(order, lengths, weight, values, earlier)


def sum_kernel(length_ref, terms_ref, earlier_ref, out_ref, done_ref):
    done_ref[...] = earlier_ref[...]
    summed = terms_ref[0]
    for n in range(1, terms_ref.shape[0]):
        summed = summed + terms_ref[n]
    positions = lax.broadcasted_iota(jnp.int32, summed.shape, 1)
    summed = jnp.where(positions < length_ref[0], summed, 0.0).astype(jnp.bfloat16)
    for n in range(out_ref.shape[0]):
        out_ref[n] = summed


def sum_terms(terms, length, copies, earlier):
    return pl.pallas_call(
        sum_kernel,
        grid=(1,),
        in_specs=[pl.BlockSpec(memory_space=pltpu.SMEM), whole(terms.shape), whole(earlier.shape)],
        out_specs=[whole((copies,) + terms.shape[1:]), whole(earlier.shape)],
        out_shape=[
            jax.ShapeDtypeStruct((copies,) + terms.shape[1:], jnp.bfloat16),
            jax.ShapeDtypeStruct(earlier.shape, earlier.dtype),
        ],
        name="sum_terms",
    )(length, terms, earlier)


def digits_kernel(
    place_ref, near_ref, far_ref, own_ref, other_ref, earlier_ref, digits_ref, scale_ref, turned
):
    group, core = place_ref[0], place_ref[1]
    examples = own_ref.shape[0]
    half = examples // 2
    for e in range(2 * examples):
        g, example = e // examples, e % examples
        values = jnp.where(group == g, own_ref[example], other_ref[example])
        slot = g * half + example % half
        hidden = jnp.where(core == example // half, near_ref[slot], far_ref[slot])
        grads = lax.dot_general(
            hidden, values, (((1,), (1,)), ((), ())), preferred_element_type=jnp.float32
        )
        turned[:, e, :] = grads.astype(jnp.bfloat16).astype(jnp.float32)
    values = turned[...]
    largest = jnp.max(jnp.max(jnp.abs(values), axis=0), axis=1, keepdims=True)
    largest = jnp.maximum(largest, 1e-30)
    rest = values * (DIGIT_TOP / largest)[None]
    digits = []
    for _ in range(DIGITS):
        digit = jnp.round(rest)
        digits.append(digit)
        rest = (rest - digit) * DIGIT_STEP
    digits_ref[...] = jnp.concatenate(digits, axis=1).astype(F8)
    scale_ref[...] = largest * (1 / DIGIT_TOP)


def gradient_digits(near, far, values, other, place, earlier):
    columns = near.shape[1]
    examples, rows, tokens = other.shape
    lines = 2 * examples
    return pl.pallas_call(
        digits_kernel,
        grid_spec=pltpu.PrefetchScalarGridSpec(
            num_scalar_prefetch=1,
            grid=(1,),
            in_specs=[
                whole(near.shape),
                whole(near.shape),
                pl.BlockSpec(other.shape, lambda _, place: (0, place[0], 0)),
                whole(other.shape),
                whole(earlier.shape),
            ],
            out_specs=[whole((columns, DIGITS * lines, rows)), whole((lines, 1))],
            scratch_shapes=[pltpu.VMEM((columns, lines, rows), jnp.float32)],
        ),
        out_shape=[
            jax.ShapeDtypeStruct((columns, DIGITS * lines, rows), F8),
            jax.ShapeDtypeStruct((lines, 1), jnp.float32),
        ],
        compiler_params=pltpu.CompilerParams(vmem_limit_bytes=28 << 20),
        name="gradient_digits",
    )(place, near, far, values, other, earlier)


def hash_bytes(seeds, group, block):
    columns = lax.broadcasted_iota(jnp.int32, (seeds.shape[0], PROJECTED_BLOCK), 1)
    words = scramble((seeds + (group * PROJECTED_DIMS + block * PROJECTED_BLOCK)) + columns)
    found = []
    for byte in range(4):
        shifted = lax.shift_right_logical(words, jnp.full_like(words, 8 * byte)) if byte else words
        found.append(shifted.astype(jnp.int8))
    return found


def project_kernel(
    first_group, seeds_ref, digits_ref, scale_ref, before_ref, earlier_ref, out_ref, done_ref, total
):
    block, group = pl.program_id(0), pl.program_id(1)

    @pl.when(group == 0)
    def _():
        total[...] = jnp.zeros_like(total)
        done_ref[...] = scale_ref[...]

    found = hash_bytes(seeds_ref[...], first_group + group, block)
    signs = []
    for byte in range(4):
        for bit in range(8):
            is_set = (found[byte] & jnp.int8((1 << bit) - 256 * (bit == 7))) != 0
            signs.append(jnp.where(is_set, F8(-1), F8(1)))
    digits = jnp.concatenate([digits_ref[c] for c in range(32)], axis=1)
    total[...] += jnp.dot(
        digits, jnp.concatenate(signs, axis=0), preferred_element_type=jnp.float32
    )

    @pl.when(group == pl.num_programs(1) - 1)
    def _():
        examples = out_ref.shape[0]
        added = total[(DIGITS - 1) * examples :, :]
        for digit in reversed(range(DIGITS - 1)):
            added = added * (1 / DIGIT_STEP) + total[digit * examples : (digit + 1) * examples, :]
        out_ref[...] = before_ref[...] + added * scale_ref[...]


def project(seeds, digits, scale, before, first_group, skipped, groups, earlier):
    lines, rows = digits.shape[1:]
    examples = scale.shape[0]
    return pl.pallas_call(
        functools.partial(project_kernel, first_group + skipped),
        grid=(PROJECTED_DIMS // PROJECTED_BLOCK, groups),
        in_specs=[
            whole(seeds.shape),
            pl.BlockSpec((32, lines, rows), lambda k, g: (g + skipped, 0, 0)),
            whole((examples, 1)),
            pl.BlockSpec((examples, PROJECTED_BLOCK), lambda k, g: (0, k)),
            whole(earlier.shape),
        ],
        out_specs=[
            pl.BlockSpec((examples, PROJECTED_BLOCK), lambda k, g: (0, k)),
            whole((examples, 1)),
        ],
        out_shape=[
            jax.ShapeDtypeStruct((examples, PROJECTED_DIMS), jnp.float32),
            jax.ShapeDtypeStruct((examples, 1), jnp.float32),
        ],
        scratch_shapes=[pltpu.VMEM((lines, PROJECTED_BLOCK), jnp.float32)],
        cost_estimate=pl.CostEstimate(
            flops=2 * 256 * 32 * groups * rows * PROJECTED_DIMS, bytes_accessed=digits.size, transcendentals=0
        ),
        compiler_params=pltpu.CompilerParams(vmem_limit_bytes=32 << 20),
        name="project",
    )(seeds, digits, scale, before, earlier)


def shards(
    acts,
    output_gradients,
    adapter_down,
    adapter_up,
    lengths,
    sign_hash_seed,
    tile_indices,
    validation_projected,
    parts=2,
    chips=8,
):
    examples, width, tokens = acts.shape
    devices = 2 * chips
    half_examples = examples // 2
    group, chip, core = (lax.axis_index(name).astype(jnp.int32) for name in ("groups", "chip", "core"))
    place = jnp.stack([group, core])
    order = (jnp.arange(examples, dtype=jnp.int32) + (1 - core) * half_examples) % examples

    rank = adapter_down.shape[0]
    weights = (adapter_up, adapter_down)
    inputs = (output_gradients, acts)
    length = jnp.take(lengths, core * half_examples + chip * half_examples // chips).reshape(1)

    row_seeds = scramble(tile_indices + scramble(sign_hash_seed[0]))
    row_seeds = lax.dynamic_slice_in_dim(row_seeds, group * (width // 2), width // 2, 0)[:, None]

    def halves(values):
        sent = lax.dynamic_slice_in_dim(values, (1 - group) * (width // 2), width // 2, 1)
        return values, lax.ppermute(sent, "groups", [(0, 1), (1, 0)])

    def own_terms(half, earlier):
        sent, kept, done = partial_hidden(inputs[half], weights[half], lengths, order, half == 0, earlier)
        return kept + lax.ppermute(sent, "core", [(0, 1), (1, 0)]), done

    def exchange(terms):
        rows = terms.shape[0] * terms.shape[1] // chips
        return lax.all_to_all(terms.reshape(chips, rows, tokens), "chip", 0, 0, tiled=True)

    def spread(terms, earlier):
        copies, done = sum_terms(terms, length, parts * chips, earlier)
        near = lax.all_to_all(copies, ("groups", "chip"), 0, 0, tiled=True)
        return near.reshape(parts * half_examples, rank, tokens), done

    def digits_of(values, near, earlier):
        far = lax.ppermute(near, "core", [(0, 1), (1, 0)])
        return gradient_digits(near, far, *values, place, earlier)

    groups = rank // 32
    total = jnp.zeros((parts * examples, PROJECTED_DIMS), jnp.float32)
    terms, done = own_terms(0, order.reshape(1, examples))
    terms = exchange(terms)
    acts_halves = halves(acts)
    summed, done = spread(terms, done)
    terms, _ = own_terms(1, acts_halves[1][0, :8, :128])
    gradients_halves = halves(output_gradients)
    digits, scale = digits_of(acts_halves, summed, done)
    terms = exchange(after(terms, scale))
    total, done = project(row_seeds, digits, scale, total, 0, 0, 2, scale)
    summed, _ = spread(terms, done)
    total, done = project(row_seeds, digits, scale, total, 0, 2, groups - 2, scale)
    digits, scale = digits_of(gradients_halves, after(summed, done), done)
    projected, _ = project(row_seeds, digits, scale, total, groups, 0, groups, scale)

    local_k = validation_projected.shape[1]
    sent = projected.reshape(parts, examples, devices, local_k).transpose(0, 2, 1, 3)
    sent = sent.reshape(parts * devices, examples, local_k)
    own = lax.all_to_all(sent, ("groups", "chip", "core"), 0, 0, tiled=True).sum(0)

    inner = jnp.einsum("ek,vk->ev", own, validation_projected, precision=lax.Precision.HIGHEST)
    val_sq = jnp.sum(validation_projected * validation_projected, 1)
    train_sq = jnp.sum(own * own, 1)
    packed = jnp.concatenate(
        [inner, val_sq[None, :], jnp.pad(train_sq, (0, inner.shape[1] - examples))[None, :]], 0
    )
    packed = jnp.pad(packed, ((0, -packed.shape[0] % 8), (0, 0)))
    summed = lax.all_to_all(
        jnp.broadcast_to(packed[None], (devices,) + packed.shape), ("chip", "core"), 0, 0, tiled=True
    ).sum(0)
    train_norm = jnp.sqrt(summed[examples + 1, :examples] + 1e-06)
    val_norm = jnp.sqrt(summed[examples] + 1e-06)
    factor = math.sqrt(PROJECTED_DIMS)
    unit_grads = own * (factor / train_norm)[:, None]
    alignment = factor * summed[:examples] / (train_norm[:, None] * val_norm[None, :])
    task_score = jnp.mean(alignment.reshape(examples, TASKS, -1), 2)
    return (unit_grads, alignment, task_score)


def solution(mesh):
    groups, devices = mesh.shape["groups"], mesh.shape["mp"]
    chips = devices // 2
    mesh = Mesh(mesh.devices.reshape(groups, chips, 2), ("groups", "chip", "core"))
    split = ("chip", "core")
    placed = (
        P("groups", split, None),
        P("groups", split, None),
        P(None, split),
        P(split, None),
        P("groups"),
        P(),
        P(split),
        P("groups", split),
    )
    return jax.shard_map(
        functools.partial(shards, parts=groups, chips=chips),
        mesh=mesh,
        in_specs=placed,
        out_specs=(P("groups", split), P("groups", None), P("groups", None)),
        check_vma=False,
    )
```

```python
import functools
import math

import jax
import jax.numpy as jnp
from jax import lax
from jax.experimental import pallas as pl
from jax.experimental.pallas import tpu as pltpu
from jax.sharding import Mesh
from jax.sharding import PartitionSpec as P

PROJECTED_DIMS = 8192
TASKS = 4
DIGITS = 4
DIGIT_STEP = 16.0
DIGIT_TOP = 8.0
F8 = jnp.float8_e4m3fn
PROJECTED_BLOCK = 2048


def scramble(hashed):
    hashed = hashed ^ lax.shift_right_logical(hashed, jnp.full_like(hashed, 16))
    hashed = hashed * jnp.int32(2146121005)
    hashed = hashed ^ lax.shift_right_logical(hashed, jnp.full_like(hashed, 15))
    hashed = hashed * jnp.int32(-2073254261)
    hashed = hashed ^ lax.shift_right_logical(hashed, jnp.full_like(hashed, 16))
    return hashed


def whole(shape):
    return pl.BlockSpec(shape, lambda *_: (0,) * len(shape))


def after(value, earlier):
    return pl.pallas_call(
        lambda value_ref, earlier_ref, out_ref: None,
        grid=(1,),
        in_specs=[pl.BlockSpec(memory_space=pl.ANY), whole(earlier.shape)],
        out_specs=pl.BlockSpec(memory_space=pl.ANY),
        out_shape=jax.ShapeDtypeStruct(value.shape, value.dtype),
        input_output_aliases={0: 0},
        name="after",
    )(value, earlier)


def add_kernel(kept_ref, received_ref, earlier_ref, out_ref):
    out_ref[...] = kept_ref[...] + received_ref[...]


def add_terms(kept, received, earlier):
    return pl.pallas_call(
        add_kernel,
        grid=(kept.shape[0],),
        in_specs=[pl.BlockSpec((1,) + kept.shape[1:], lambda e: (e, 0, 0))] * 2 + [whole(earlier.shape)],
        out_specs=pl.BlockSpec((1,) + kept.shape[1:], lambda e: (e, 0, 0)),
        out_shape=jax.ShapeDtypeStruct(kept.shape, kept.dtype),
        name="add_terms",
    )(kept, received, earlier)


def sender_order(step, place, examples):
    return lax.rem(step + (1 - place[1]) * (examples // 2), examples)


def hidden_kernel(masked, follows, place_ref, lengths_ref, weight_ref, values_ref, *rest):
    step = pl.program_id(0)
    if follows:
        earlier_ref, passed_ref, copied_ref, sent_ref, kept_ref, done_ref = rest
        copied_ref[...] = passed_ref[...]
    else:
        sent_ref, kept_ref, done_ref = rest
    product = lax.dot_general(
        weight_ref[...],
        values_ref[0],
        (((0 if masked else 1,), (0,)), ((), ())),
        preferred_element_type=jnp.float32,
    )
    if masked:
        positions = lax.broadcasted_iota(jnp.int32, product.shape, 1)
        example = sender_order(step, place_ref, pl.num_programs(0))
        product = jnp.where(positions < lengths_ref[example], product, 0.0)
    early = step < pl.num_programs(0) // 2

    @pl.when(early)
    def _():
        sent_ref[0] = product

    @pl.when(jnp.logical_not(early))
    def _():
        kept_ref[0] = product

    done_ref[...] = jnp.zeros_like(done_ref)


def partial_hidden(values, weight, lengths, place, masked, earlier=None, passed=None):
    examples, width, tokens = values.shape
    count = weight.shape[1 if masked else 0]
    half = examples // 2
    rows = width // 2
    follows = earlier is not None
    in_specs = [
        pl.BlockSpec(memory_space=pltpu.SMEM),
        whole(weight.shape),
        pl.BlockSpec((1, width, tokens), lambda e, place: (sender_order(e, place, examples), 0, 0)),
    ]
    out_specs = [
        pl.BlockSpec((1, count, tokens), lambda e, place: (jnp.minimum(e, half - 1), 0, 0)),
        pl.BlockSpec((1, count, tokens), lambda e, place: (jnp.maximum(e - half, 0), 0, 0)),
        whole((8, 1)),
    ]
    shape = jax.ShapeDtypeStruct((half, count, tokens), jnp.float32)
    out_shape = [shape, shape, jax.ShapeDtypeStruct((8, 1), jnp.float32)]
    operands = [place, lengths, weight, values]
    if follows:
        in_specs += [
            whole(earlier.shape),
            pl.BlockSpec((1, rows, tokens), lambda e, place: (e, 1 - place[0], 0)),
        ]
        out_specs = [pl.BlockSpec((1, rows, tokens), lambda e, place: (e, 0, 0))] + out_specs
        out_shape = [jax.ShapeDtypeStruct((examples, rows, tokens), passed.dtype)] + out_shape
        operands += [earlier, passed]
    return pl.pallas_call(
        functools.partial(hidden_kernel, masked, follows),
        grid_spec=pltpu.PrefetchScalarGridSpec(
            num_scalar_prefetch=1, grid=(examples,), in_specs=in_specs, out_specs=out_specs
        ),
        out_shape=out_shape,
        name="partial_hidden",
    )(*operands)


def sum_kernel(length_ref, terms_ref, earlier_ref, out_ref, done_ref):
    done_ref[...] = earlier_ref[...]
    summed = terms_ref[0]
    for n in range(1, terms_ref.shape[0]):
        summed = summed + terms_ref[n]
    positions = lax.broadcasted_iota(jnp.int32, summed.shape, 1)
    summed = jnp.where(positions < length_ref[0], summed, 0.0).astype(jnp.bfloat16)
    for n in range(out_ref.shape[0]):
        out_ref[n] = summed


def sum_terms(terms, length, copies, earlier):
    return pl.pallas_call(
        sum_kernel,
        grid=(1,),
        in_specs=[pl.BlockSpec(memory_space=pltpu.SMEM), whole(terms.shape), whole(earlier.shape)],
        out_specs=[whole((copies,) + terms.shape[1:]), whole(earlier.shape)],
        out_shape=[
            jax.ShapeDtypeStruct((copies,) + terms.shape[1:], jnp.bfloat16),
            jax.ShapeDtypeStruct(earlier.shape, earlier.dtype),
        ],
        name="sum_terms",
    )(length, terms, earlier)


def digits_kernel(
    place_ref, near_ref, far_ref, own_ref, other_ref, earlier_ref, digits_ref, scale_ref, turned
):
    group, core = place_ref[0], place_ref[1]
    examples = own_ref.shape[0]
    half = examples // 2
    for e in range(2 * examples):
        g, example = e // examples, e % examples
        values = jnp.where(group == g, own_ref[example], other_ref[example])
        slot = g * half + example % half
        hidden = jnp.where(core == example // half, near_ref[slot], far_ref[slot])
        grads = lax.dot_general(
            hidden, values, (((1,), (1,)), ((), ())), preferred_element_type=jnp.float32
        )
        turned[:, e, :] = grads.astype(jnp.bfloat16).astype(jnp.float32)
    values = turned[...]
    largest = jnp.max(jnp.max(jnp.abs(values), axis=0), axis=1, keepdims=True)
    largest = jnp.maximum(largest, 1e-30)
    rest = values * (DIGIT_TOP / largest)[None]
    digits = []
    for _ in range(DIGITS):
        digit = jnp.round(rest)
        digits.append(digit)
        rest = (rest - digit) * DIGIT_STEP
    digits_ref[...] = jnp.concatenate(digits, axis=1).astype(F8)
    scale_ref[...] = largest * (1 / DIGIT_TOP)


def gradient_digits(near, far, values, other, place, earlier):
    columns = near.shape[1]
    examples, rows, tokens = other.shape
    lines = 2 * examples
    return pl.pallas_call(
        digits_kernel,
        grid_spec=pltpu.PrefetchScalarGridSpec(
            num_scalar_prefetch=1,
            grid=(1,),
            in_specs=[
                whole(near.shape),
                whole(near.shape),
                pl.BlockSpec(other.shape, lambda _, place: (0, place[0], 0)),
                whole(other.shape),
                whole(earlier.shape),
            ],
            out_specs=[whole((columns, DIGITS * lines, rows)), whole((lines, 1))],
            scratch_shapes=[pltpu.VMEM((columns, lines, rows), jnp.float32)],
        ),
        out_shape=[
            jax.ShapeDtypeStruct((columns, DIGITS * lines, rows), F8),
            jax.ShapeDtypeStruct((lines, 1), jnp.float32),
        ],
        compiler_params=pltpu.CompilerParams(vmem_limit_bytes=28 << 20),
        name="gradient_digits",
    )(place, near, far, values, other, earlier)


def hash_bytes(seeds, group, block):
    columns = lax.broadcasted_iota(jnp.int32, (seeds.shape[0], PROJECTED_BLOCK), 1)
    words = scramble((seeds + (group * PROJECTED_DIMS + block * PROJECTED_BLOCK)) + columns)
    found = []
    for byte in range(4):
        shifted = lax.shift_right_logical(words, jnp.full_like(words, 8 * byte)) if byte else words
        found.append(shifted.astype(jnp.int8))
    return found


def project_kernel(
    first_group, seeds_ref, digits_ref, scale_ref, before_ref, earlier_ref, out_ref, done_ref, total
):
    block, group = pl.program_id(0), pl.program_id(1)

    @pl.when(group == 0)
    def _():
        total[...] = jnp.zeros_like(total)
        done_ref[...] = scale_ref[...]

    found = hash_bytes(seeds_ref[...], first_group + group, block)
    signs = []
    for byte in range(4):
        for bit in range(8):
            is_set = (found[byte] & jnp.int8((1 << bit) - 256 * (bit == 7))) != 0
            signs.append(jnp.where(is_set, F8(-1), F8(1)))
    digits = jnp.concatenate([digits_ref[c] for c in range(32)], axis=1)
    total[...] += jnp.dot(
        digits, jnp.concatenate(signs, axis=0), preferred_element_type=jnp.float32
    )

    @pl.when(group == pl.num_programs(1) - 1)
    def _():
        examples = out_ref.shape[0]
        added = total[(DIGITS - 1) * examples :, :]
        for digit in reversed(range(DIGITS - 1)):
            added = added * (1 / DIGIT_STEP) + total[digit * examples : (digit + 1) * examples, :]
        out_ref[...] = before_ref[...] + added * scale_ref[...]


def project(seeds, digits, scale, before, first_group, skipped, groups, earlier):
    lines, rows = digits.shape[1:]
    examples = scale.shape[0]
    return pl.pallas_call(
        functools.partial(project_kernel, first_group + skipped),
        grid=(PROJECTED_DIMS // PROJECTED_BLOCK, groups),
        in_specs=[
            whole(seeds.shape),
            pl.BlockSpec((32, lines, rows), lambda k, g: (g + skipped, 0, 0)),
            whole((examples, 1)),
            pl.BlockSpec((examples, PROJECTED_BLOCK), lambda k, g: (0, k)),
            whole(earlier.shape),
        ],
        out_specs=[
            pl.BlockSpec((examples, PROJECTED_BLOCK), lambda k, g: (0, k)),
            whole((examples, 1)),
        ],
        out_shape=[
            jax.ShapeDtypeStruct((examples, PROJECTED_DIMS), jnp.float32),
            jax.ShapeDtypeStruct((examples, 1), jnp.float32),
        ],
        scratch_shapes=[pltpu.VMEM((lines, PROJECTED_BLOCK), jnp.float32)],
        cost_estimate=pl.CostEstimate(
            flops=2 * 256 * 32 * groups * rows * PROJECTED_DIMS, bytes_accessed=digits.size, transcendentals=0
        ),
        compiler_params=pltpu.CompilerParams(vmem_limit_bytes=32 << 20),
        name="project",
    )(seeds, digits, scale, before, earlier)


def shards(
    acts,
    output_gradients,
    adapter_down,
    adapter_up,
    lengths,
    sign_hash_seed,
    tile_indices,
    validation_projected,
    parts=2,
    chips=8,
):
    examples, width, tokens = acts.shape
    devices = 2 * chips
    half_examples = examples // 2
    group, chip, core = (lax.axis_index(name).astype(jnp.int32) for name in ("groups", "chip", "core"))
    place = jnp.stack([group, core])
    rank = adapter_down.shape[0]
    length = jnp.take(lengths, core * half_examples + chip * half_examples // chips).reshape(1)

    row_seeds = scramble(tile_indices + scramble(sign_hash_seed[0]))
    row_seeds = lax.dynamic_slice_in_dim(row_seeds, group * (width // 2), width // 2, 0)[:, None]

    def swap(values, name):
        return lax.ppermute(values, name, [(0, 1), (1, 0)])

    def exchange(terms):
        rows = terms.shape[0] * terms.shape[1] // chips
        return lax.all_to_all(terms.reshape(chips, rows, tokens), "chip", 0, 0, tiled=True)

    def spread(terms, earlier):
        copies, done = sum_terms(terms, length, parts * chips, earlier)
        near = lax.all_to_all(copies, ("groups", "chip"), 0, 0, tiled=True)
        return near.reshape(parts * half_examples, rank, tokens), done

    def digits_of(values, near, earlier):
        far = swap(near, "core")
        return gradient_digits(near, far, *values, place, earlier)

    groups = rank // 32
    total = jnp.zeros((parts * examples, PROJECTED_DIMS), jnp.float32)
    sent, kept, done = partial_hidden(output_gradients, adapter_up, lengths, place, True)
    terms = exchange(kept + swap(sent, "core"))
    acts_sent = lax.dynamic_slice_in_dim(acts, (1 - group) * (width // 2), width // 2, 1)
    acts_other = swap(acts_sent, "groups")
    summed, done = spread(terms, done)
    gradients_sent, sent, kept, _ = partial_hidden(
        acts, adapter_down, lengths, place, False, acts_other[0, :8, :128], output_gradients
    )
    gradients_other = swap(gradients_sent, "groups")
    received = swap(sent, "core")
    digits, scale = digits_of((acts, acts_other), summed, received[0, :8, :128])
    terms = exchange(add_terms(kept, received, scale))
    total, done = project(row_seeds, digits, scale, total, 0, 0, 2, scale)
    summed, _ = spread(terms, done)
    total, done = project(row_seeds, digits, scale, total, 0, 2, groups - 2, scale)
    digits, scale = digits_of((output_gradients, gradients_other), after(summed, done), done)
    projected, _ = project(row_seeds, digits, scale, total, groups, 0, groups, scale)

    local_k = validation_projected.shape[1]
    sent = projected.reshape(parts, examples, devices, local_k).transpose(0, 2, 1, 3)
    sent = sent.reshape(parts * devices, examples, local_k)
    own = lax.all_to_all(sent, ("groups", "chip", "core"), 0, 0, tiled=True).sum(0)

    inner = jnp.einsum("ek,vk->ev", own, validation_projected, precision=lax.Precision.HIGHEST)
    val_sq = jnp.sum(validation_projected * validation_projected, 1)
    train_sq = jnp.sum(own * own, 1)
    packed = jnp.concatenate(
        [inner, val_sq[None, :], jnp.pad(train_sq, (0, inner.shape[1] - examples))[None, :]], 0
    )
    packed = jnp.pad(packed, ((0, -packed.shape[0] % 8), (0, 0)))
    summed = lax.all_to_all(
        jnp.broadcast_to(packed[None], (devices,) + packed.shape), ("chip", "core"), 0, 0, tiled=True
    ).sum(0)
    train_norm = jnp.sqrt(summed[examples + 1, :examples] + 1e-06)
    val_norm = jnp.sqrt(summed[examples] + 1e-06)
    factor = math.sqrt(PROJECTED_DIMS)
    unit_grads = own * (factor / train_norm)[:, None]
    alignment = factor * summed[:examples] / (train_norm[:, None] * val_norm[None, :])
    task_score = jnp.mean(alignment.reshape(examples, TASKS, -1), 2)
    return (unit_grads, alignment, task_score)


def solution(mesh):
    groups, devices = mesh.shape["groups"], mesh.shape["mp"]
    chips = devices // 2
    mesh = Mesh(mesh.devices.reshape(groups, chips, 2), ("groups", "chip", "core"))
    split = ("chip", "core")
    placed = (
        P("groups", split, None),
        P("groups", split, None),
        P(None, split),
        P(split, None),
        P("groups"),
        P(),
        P(split),
        P("groups", split),
    )
    return jax.shard_map(
        functools.partial(shards, parts=groups, chips=chips),
        mesh=mesh,
        in_specs=placed,
        out_specs=(P("groups", split), P("groups", None), P("groups", None)),
        check_vma=False,
    )
```
